32 devices in a mesh: wide: 8 (over y, x, core), blk: 4 (over z).
Axes of the slice: x: 2, y: 2, z: 4, core: 2. Of those that a mesh axis runs over, the one named last changes fastest.
Arguments:
- tokens: bfloat16 [16384, 8192], P(('wide', 'blk')), may hold values from -6 to 6
- base_key_matrix: bfloat16 [8192, 1024], P('blk'), may hold values from -0.0625 to 0.0625
- adapter_down_weights: bfloat16 [256, 64, 8192], P(('wide', 'blk')), may hold values from -0.0625 to 0.0625
- adapter_up_weights: bfloat16 [256, 64, 1024], P(('wide', 'blk')), may hold values from -0.75 to 0.75
- request_adapter_index: int32 [256], P(('wide', 'blk')), may hold values from 0 to 255, as said below
Outputs:
- keys: bfloat16 [16384, 1024], P(('wide', 'blk'))
The draws below stay inside these ranges and needn't reach their ends.
Inputs may be any that keep to these rules, and one draw needn't show every extreme that they name: `request_adapter_index`: request r lies on device r // 8 of wide+blk; adapter a lies on device a // 8. Each request's adapter lies on a device with the same blk index as the request. Of one device's requests at most 2 have adapters on any one wide index; for every blk index one wide index holds the adapters of exactly 2 requests of every device with that blk index.
All inputs are finite; a program needn't handle non-finite values.
Results may differ from the reference program's by a relative error of at most 0.005.
Values may be sent and summed in bfloat16 or wider, within the bound.
A program may use at most 192 MiB of HBM per device.

```python
import jax
import jax.numpy as jnp
from jax import lax

MODEL_WIDTH = 8192
KEY_FEATURES = 1024
ADAPTER_RANK = 64
SEQ = 64
ADP_DEV = 8
REQ_DEV = 8
CAP = 2
ADAPTER_COUNT = 256
REQUESTS = 256
TOKENS = 16384
N_WIDE = 8
N_BLK = 4


def draw_request_adapter_index(key, part):
    hot_key, rest_key = jax.random.split(key)
    hottest = jax.random.randint(hot_key, (N_BLK,), 0, N_WIDE)
    device_keys = jax.random.split(rest_key, N_WIDE * N_BLK)

    def per_device(device_key, device):
        column = device % N_BLK
        first_key, second_key, third_key = jax.random.split(device_key, 3)
        others = jax.random.permutation(first_key, N_WIDE - 1).astype(jnp.int32)
        hot_owner = hottest[column].astype(jnp.int32)
        rest = (hot_owner + 1 + others) % N_WIDE
        owners = jnp.concatenate([jnp.full((CAP,), hot_owner, jnp.int32), rest])[:REQ_DEV]
        owners = owners[jax.random.permutation(second_key, REQ_DEV)]
        local = jax.random.randint(third_key, (REQ_DEV,), 0, ADP_DEV)
        return ((owners * N_BLK + column) * ADP_DEV + local).astype(jnp.int32)
    devices = jnp.arange(N_WIDE * N_BLK, dtype=jnp.int32)
    return jax.vmap(per_device)(device_keys, devices).reshape(REQUESTS)


def block_levels(own_key, dims, pieces, smallest, top_value):
    def one(position, blocks):
        heights = jax.random.uniform(jax.random.fold_in(jax.random.fold_in(own_key, 6), position), (blocks,), jnp.float32, smallest / len(pieces), top_value / len(pieces))
        return jnp.repeat(jnp.exp(heights), dims[position] // blocks).reshape((-1,) + (1,) * (len(dims) - position - 1))

    factor_of = one(*pieces[0])
    for cut in pieces[1:]:
        factor_of = factor_of * one(*cut)
    return factor_of


def centred(own_key, dims, spread, reach, cuts=(), kind=jnp.bfloat16):
    level = block_levels(own_key, dims, cuts, -0.22, 0.18) if cuts else 1.0
    values = jax.random.normal(own_key, dims, jnp.float32) * spread * level
    return jnp.minimum(jnp.maximum(values, -reach), reach).astype(kind)


def setup_inputs(seed: int = 0) -> dict:
    arg_keys = jax.random.split(jax.random.key(seed), 6)
    return {
        "tokens": centred(arg_keys[0], (TOKENS, MODEL_WIDTH), 1.0, 6.0, ((0, 32),)),
        "base_key_matrix": centred(arg_keys[1], (MODEL_WIDTH, KEY_FEATURES), MODEL_WIDTH ** -0.5, 0.0625, ((0, 4),)),
        "adapter_down_weights": centred(arg_keys[2], (ADAPTER_COUNT, ADAPTER_RANK, MODEL_WIDTH), MODEL_WIDTH ** -0.5, 0.0625, ((0, 32),)),
        "adapter_up_weights": centred(arg_keys[3], (ADAPTER_COUNT, ADAPTER_RANK, KEY_FEATURES), ADAPTER_RANK ** -0.5, 0.75, ((0, 32),)),
        "request_adapter_index": draw_request_adapter_index(jax.random.fold_in(arg_keys[5], 71), 0),
    }


def reference(tokens, base_key_matrix, adapter_down_weights, adapter_up_weights, request_adapter_index):
    base = jnp.dot(tokens, base_key_matrix, preferred_element_type=jnp.float32)
    requests = tokens.reshape(REQUESTS, SEQ, MODEL_WIDTH)

    def one_request(args):
        rows, adapter_index = args
        down_projection = lax.dynamic_index_in_dim(adapter_down_weights, adapter_index, 0, keepdims=False)
        up_projection = lax.dynamic_index_in_dim(adapter_up_weights, adapter_index, 0, keepdims=False)
        shrink = jnp.dot(rows, down_projection.T, preferred_element_type=jnp.float32).astype(jnp.bfloat16)
        return jnp.dot(shrink, up_projection, preferred_element_type=jnp.float32).astype(jnp.bfloat16)

    deltas = lax.map(one_request, (requests, request_adapter_index))
    return (base + deltas.reshape(TOKENS, KEY_FEATURES).astype(jnp.float32)).astype(jnp.bfloat16)
```

```python
import functools

import jax
import jax.numpy as jnp
from jax import lax
from jax.experimental import pallas as pl
from jax.experimental.pallas import tpu as pltpu
from jax.sharding import PartitionSpec as P

SEQ = 64
CAP = 2
MESH = pl.DeviceIdType.MESH
F32 = jnp.float32
BF16 = jnp.bfloat16


def take_kernel(_, x_ref, o_ref):
    o_ref[...] = x_ref[...]


def take(x, index):
    block = (1,) + x.shape[1:]
    return pl.pallas_call(
        take_kernel,
        grid_spec=pltpu.PrefetchScalarGridSpec(
            num_scalar_prefetch=1,
            grid=(index.shape[0],),
            in_specs=[pl.BlockSpec(block, lambda i, index_ref: (index_ref[i], 0, 0))],
            out_specs=pl.BlockSpec(block, lambda i, index_ref: (i, 0, 0)),
        ),
        out_shape=jax.ShapeDtypeStruct((index.shape[0],) + x.shape[1:], x.dtype),
    )(index, x)


def routing(index, resident_count, block_count):
    owner = index // (resident_count * block_count)
    local = index % resident_count
    positions = jnp.arange(index.shape[-1], dtype=jnp.int32)
    same = owner[..., :, None] == owner[..., None, :]
    earlier = positions[None, :] < positions[:, None]
    rank = jnp.sum(jnp.where(same & earlier, 1, 0), axis=-1).astype(jnp.int32)
    return owner, local, rank


def padded_path(tokens, weight, down, up, index):
    wide_count = lax.axis_size("wide")
    req_count = index.shape[0]
    owner, local, rank = routing(index, down.shape[0], lax.axis_size("blk"))
    slot_count = wide_count * CAP
    base = jnp.dot(
        tokens,
        lax.all_gather(weight, "blk", axis=0, tiled=True),
        preferred_element_type=F32,
    )
    positions = jnp.arange(req_count, dtype=jnp.int32)
    slot_of_req = owner * CAP + rank
    member = slot_of_req[:, None] == jnp.arange(slot_count, dtype=jnp.int32)[None, :]
    source_req = jnp.sum(jnp.where(member, positions[:, None], 0), axis=0)
    slot_local = jnp.sum(jnp.where(member, local[:, None], 0), axis=0)[:, None]
    outgoing = take(tokens.reshape(req_count, SEQ, tokens.shape[1]), source_req)
    arrived = lax.all_to_all(outgoing, "wide", split_axis=0, concat_axis=0, tiled=True)
    ids = lax.all_to_all(slot_local, "wide", split_axis=0, concat_axis=0, tiled=True)[:, 0]
    shrink = jnp.einsum(
        "sqd,srd->sqr", arrived, take(down, ids), preferred_element_type=F32
    ).astype(BF16)
    expand = jnp.einsum(
        "sqr,srk->sqk", shrink, take(up, ids), preferred_element_type=F32
    ).astype(BF16)
    returned = lax.all_to_all(expand, "wide", split_axis=0, concat_axis=0, tiled=True)
    delta = take(returned, slot_of_req).reshape(tokens.shape[0], up.shape[2])
    return (base + delta.astype(F32)).astype(BF16)


def fused_kernel(
    n, m,
    ids_ref, slot_ref, tokens_hbm, pack_hbm, weight_hbm, down_hbm, up_hbm,
    out_ref,
    tokens, weight, down, up, arrived, total, delta, returned,
    local_sem, rx_send, rx_recv, fwd_send, ret_send, ret_recv,
    own_send, chain_send, chain_recv, mate_send, mate_recv,
):
    w, p = lax.axis_index("wide"), lax.axis_index("blk")
    depth = weight_hbm.shape[0]
    half = depth // 2
    width, columns = tokens.shape[1], out_ref.shape[1]
    reqs = slot_ref.shape[0]
    core = lax.rem(w, 2)

    def partner(j):
        bits = [lax.rem(w // (1 << i), 2) for i in range((n - 1).bit_length())]
        return sum(
            ((1 - bit) if (j >> i) & 1 else bit) * (1 << i) for i, bit in enumerate(bits)
        )

    mate = partner(1)

    locals_ = [
        pltpu.make_async_copy(
            weight_hbm,
            weight.at[pl.ds(pl.multiple_of(p * depth, depth), depth)],
            local_sem.at[0],
        ),
        pltpu.make_async_copy(tokens_hbm, tokens, local_sem.at[1]),
        pltpu.make_async_copy(down_hbm, down, local_sem.at[2]),
        pltpu.make_async_copy(up_hbm, up, local_sem.at[3]),
        pltpu.make_async_copy(pack_hbm.at[w], arrived.at[w], local_sem.at[4]),
        pltpu.make_async_copy(pack_hbm.at[n], arrived.at[n + w], local_sem.at[5]),
    ]

    barrier = pltpu.get_barrier_semaphore()
    for j in range(1, n):
        pl.semaphore_signal(barrier, inc=1, device_id=(partner(j), p), device_id_type=MESH)
    for q in (lax.rem(p + 1, m), lax.rem(p + m - 1, m)):
        pl.semaphore_signal(barrier, inc=1, device_id=(w, q), device_id_type=MESH)
    for copy in locals_:
        copy.start()
    pl.semaphore_wait(barrier, n + 1)

    def remote(src, dst, send, recv, device):
        return pltpu.make_async_remote_copy(
            src_ref=src, dst_ref=dst, send_sem=send, recv_sem=recv,
            device_id=device, device_id_type=MESH,
        )

    def rows(k, side):
        return pl.ds(pl.multiple_of(k * depth + side * half, half), half)

    def own_copy(q, i):
        src = weight_hbm.at[pl.ds(pl.multiple_of(core * half, half), half)]
        return remote(src, weight.at[rows(p, core)], own_send.at[i], chain_recv.at[p], (w, q))

    def chain_copy(k, q):
        ref = weight.at[rows(k, core)]
        return remote(ref, ref, chain_send.at[k], chain_recv.at[k], (w, q))

    def mate_copy(k, side):
        ref = weight.at[rows(k, side)]
        return remote(ref, ref, mate_send.at[k], mate_recv.at[k], (mate, p))

    def slot_copy(j):
        q = partner(j)
        return remote(pack_hbm.at[q], arrived.at[w], rx_send.at[j], rx_recv.at[w], (q, p))

    def over_copy(j):
        return remote(
            pack_hbm.at[n], arrived.at[n + w], rx_send.at[n + j], rx_recv.at[n + w],
            (partner(j), p),
        )

    def forward_copy(j):
        ref = arrived.at[n + partner(j)]
        return remote(ref, ref, fwd_send.at[j], rx_recv.at[n + partner(j)], (mate, p))

    def wait_rows(slot):
        remote(
            arrived.at[slot], arrived.at[slot], rx_send.at[0], rx_recv.at[slot], (mate, p)
        ).wait_recv()

    def return_copy(j, over):
        q = partner(j)
        return remote(
            delta.at[over * n + q], returned.at[over * n + w],
            ret_send.at[over * n + j], ret_recv.at[over * n + w], (q, p),
        )

    even = [j for j in range(2, n) if j % 2 == 0]
    odd = [j for j in range(2, n) if j % 2 == 1]

    @pl.when(p + 1 < m)
    def _():
        own_copy(p + 1, 0).start()

    @pl.when(p > 0)
    def _():
        own_copy(p - 1, 1).start()

    for j in even:
        over_copy(j).start()
    over_copy(1).start()
    slot_copy(1).start()
    for j in even:
        slot_copy(j).start()

    tile = 256

    def add_base(start, length):
        at = pl.ds(pl.multiple_of(start, 128), length)

        @pl.loop(0, columns // tile)
        def _(t):
            c = pl.ds(pl.multiple_of(t * tile, tile), tile)
            total[:, c] += jnp.dot(tokens[:, at], weight[at, c], preferred_element_type=F32)

    step = min(2048, width)

    def adapter(slot, out):
        a = ids_ref[slot]

        def body(c, acc):
            at = pl.ds(pl.multiple_of(c * step, step), step)
            return acc + lax.dot_general(
                arrived[slot, :, at], down[a, :, at], (((1,), (1,)), ((), ())),
                preferred_element_type=F32,
            )

        shrink = lax.fori_loop(
            0, width // step, body, jnp.zeros((SEQ, down.shape[1]), F32)
        ).astype(BF16)
        out[slot] = jnp.dot(shrink, up[a], preferred_element_type=F32).astype(BF16)

    def serve(j, over):
        adapter(over * n + partner(j), delta)
        return_copy(j, over).start()

    def chain(d):
        for exists, k, more, q in (
            (p - d >= 0, p - d, p + 1 < m, p + 1),
            (p + d < m, p + d, p > 0, p - 1),
        ):

            @pl.when(exists)
            def _():
                chain_copy(k, lax.rem(p + 1, m)).wait_recv()
                mate_copy(k, core).start()

                @pl.when(more)
                def _():
                    chain_copy(k, q).start()

    def chain_compute(d):
        for exists, k in ((p - d >= 0, p - d), (p + d < m, p + d)):

            @pl.when(exists)
            def _():
                add_base(k * depth + core * half, half)
                mate_copy(k, 1 - core).wait_recv()
                add_base(k * depth + (1 - core) * half, half)

    total[...] = jnp.zeros_like(total)
    for i in (0, 1):
        locals_[i].wait()
    add_base(p * depth, half)
    add_base(p * depth + half, half)
    for i in (2, 3, 4, 5):
        locals_[i].wait()
    adapter(w, returned)
    adapter(n + w, returned)
    wait_rows(mate)
    serve(1, 0)
    wait_rows(n + mate)
    serve(1, 1)

    chain(1)
    for j in odd:
        slot_copy(j).start()
    chain_compute(1)
    for j in even:
        wait_rows(n + partner(j))
        forward_copy(j).start()
    for j in even:
        serve(j, 1)
    if m > 2:
        chain(2)
        chain_compute(2)
    for j in odd:
        wait_rows(n + partner(j))
        serve(j, 1)
    for j in even + odd:
        wait_rows(partner(j))
        serve(j, 0)

    @pl.loop(3, m)
    def _(d):
        chain(d)
        chain_compute(d)

    for over in (0, 1):
        for j in range(1, n):
            slot = over * n + partner(j)
            remote(
                delta.at[slot], returned.at[slot], ret_send.at[0], ret_recv.at[slot], (mate, p)
            ).wait_recv()

    @pl.loop(0, reqs)
    def _(r):
        at = pl.ds(pl.multiple_of(r * SEQ, SEQ), SEQ)
        out_ref[at] = (total[at] + returned[slot_ref[r]].astype(F32)).astype(out_ref.dtype)

    @pl.when(p + 1 < m)
    def _():
        own_copy(p + 1, 0).wait_send()

    @pl.when(p > 0)
    def _():
        own_copy(p - 1, 1).wait_send()

    @pl.loop(1, m)
    def _(d):
        for exists, k, more, q in (
            (p - d >= 0, p - d, p + 1 < m, p + 1),
            (p + d < m, p + d, p > 0, p - 1),
        ):

            @pl.when(exists)
            def _():
                mate_copy(k, core).wait_send()

                @pl.when(more)
                def _():
                    chain_copy(k, q).wait_send()

    for j in range(1, n):
        slot_copy(j).wait_send()
        return_copy(j, 0).wait_send()
        return_copy(j, 1).wait_send()
    over_copy(1).wait_send()
    for j in even:
        over_copy(j).wait_send()
        forward_copy(j).wait_send()


def fused_path(tokens, weight, down, up, pack, ids, slot_of_req):
    n, m = lax.axis_size("wide"), lax.axis_size("blk")
    rows, width = tokens.shape
    columns = weight.shape[1]
    any_spec = pl.BlockSpec(memory_space=pl.ANY)
    smem = pl.BlockSpec(memory_space=pltpu.SMEM)
    dma = pltpu.SemaphoreType.DMA
    return pl.pallas_call(
        functools.partial(fused_kernel, n, m),
        out_shape=jax.ShapeDtypeStruct((rows, columns), BF16),
        in_specs=[smem, smem] + [any_spec] * 5,
        out_specs=pl.BlockSpec(memory_space=pltpu.VMEM),
        scratch_shapes=[
            pltpu.VMEM((rows, width), BF16),
            pltpu.VMEM((width, columns), BF16),
            pltpu.VMEM(down.shape, BF16),
            pltpu.VMEM(up.shape, BF16),
            pltpu.VMEM((2 * n, SEQ, width), BF16),
            pltpu.VMEM((rows, columns), F32),
            pltpu.VMEM((2 * n, SEQ, columns), BF16),
            pltpu.VMEM((2 * n, SEQ, columns), BF16),
            dma((6,)), dma((2 * n,)), dma((2 * n,)), dma((n,)), dma((2 * n,)), dma((2 * n,)),
            dma((2,)), dma((m,)), dma((m,)), dma((m,)), dma((m,)),
        ],
        compiler_params=pltpu.CompilerParams(
            collective_id=0, has_side_effects=True, vmem_limit_bytes=60 * 2**20
        ),
    )(ids, slot_of_req, tokens, pack, weight, down, up)


def per_device(tokens, weight, down, up, index):
    n, m = lax.axis_size("wide"), lax.axis_size("blk")
    w, p = lax.axis_index("wide"), lax.axis_index("blk")
    req_count = index.shape[0]
    resident = down.shape[0]
    owner, local, rank = routing(index, resident, m)
    positions = jnp.arange(req_count, dtype=jnp.int32)
    first = (owner[:, None] == jnp.arange(n, dtype=jnp.int32)) & (rank == 0)[:, None]
    source = jnp.concatenate([
        jnp.sum(jnp.where(first, positions[:, None], 0), axis=0),
        jnp.max(jnp.where(rank == 1, positions, 0))[None],
    ]).astype(jnp.int32)
    pack = take(tokens.reshape(req_count, SEQ, tokens.shape[1]), source)

    everyone = lax.all_gather(index, ("wide", "blk"), axis=0).reshape(n, m, req_count)
    owners, locals_, ranks = routing(everyone, resident, m)
    fits = jnp.all(jnp.sum(ranks, axis=-1) <= 1)
    mine = (owners == w) & (jnp.arange(m, dtype=jnp.int32) == p)[None, :, None]
    ids = jnp.concatenate([
        jnp.sum(jnp.where(mine & (ranks == k), locals_, 0), axis=(1, 2)) for k in range(CAP)
    ]).astype(jnp.int32)
    return lax.cond(
        fits,
        lambda: fused_path(tokens, weight, down, up, pack, ids, owner + n * rank),
        lambda: padded_path(tokens, weight, down, up, index),
    )


def solution(mesh):
    return jax.shard_map(
        per_device,
        mesh=mesh,
        in_specs=(
            P(("wide", "blk"), None),
            P("blk", None),
            P(("wide", "blk"), None, None),
            P(("wide", "blk"), None, None),
            P(("wide", "blk")),
        ),
        out_specs=P(("wide", "blk"), None),
        check_vma=False,
    )
```

```python
import functools

import jax
import jax.numpy as jnp
from jax import lax
from jax.experimental import pallas as pl
from jax.experimental.pallas import tpu as pltpu
from jax.sharding import PartitionSpec as P

SEQ = 64
CAP = 2
PACK_PARTS = 4
PIECES = 2
MESH = pl.DeviceIdType.MESH
F32 = jnp.float32
BF16 = jnp.bfloat16


def take_kernel(_, x_ref, o_ref):
    o_ref[...] = x_ref[...]


def take(x, index):
    block = (1,) + x.shape[1:]
    return pl.pallas_call(
        take_kernel,
        grid_spec=pltpu.PrefetchScalarGridSpec(
            num_scalar_prefetch=1,
            grid=(index.shape[0],),
            in_specs=[pl.BlockSpec(block, lambda i, index_ref: (index_ref[i], 0, 0))],
            out_specs=pl.BlockSpec(block, lambda i, index_ref: (i, 0, 0)),
        ),
        out_shape=jax.ShapeDtypeStruct((index.shape[0],) + x.shape[1:], x.dtype),
    )(index, x)


def pack_kernel(index_ref, x_ref, o_ref, held, in_sems, out_sems):
    parts, count = in_sems.shape[0], o_ref.shape[0]
    part = x_ref.shape[2] // parts
    at = [pl.ds(c * part, part) for c in range(parts)]
    arrivals = [
        pltpu.make_async_copy(x_ref.at[:, :, at[c]], held.at[:, :, at[c]], in_sems.at[c])
        for c in range(parts)
    ]
    for copy in arrivals:
        copy.start()
    copies = []
    for c in range(parts):
        arrivals[c].wait()
        for i in range(count):
            copy = pltpu.make_async_copy(
                held.at[index_ref[i], :, at[c]], o_ref.at[i, :, at[c]], out_sems.at[c, i]
            )
            copy.start()
            copies.append(copy)
    for copy in copies:
        copy.wait()


def pack_rows(x, index):
    count = index.shape[0]
    size = count * x.shape[1] * x.shape[2]
    return pl.pallas_call(
        pack_kernel,
        in_specs=[
            pl.BlockSpec(memory_space=pltpu.SMEM),
            pl.BlockSpec(memory_space=pl.ANY),
        ],
        out_specs=pl.BlockSpec(memory_space=pl.ANY),
        out_shape=jax.ShapeDtypeStruct((count,) + x.shape[1:], x.dtype),
        scratch_shapes=[
            pltpu.VMEM(x.shape, x.dtype),
            pltpu.SemaphoreType.DMA((PACK_PARTS,)),
            pltpu.SemaphoreType.DMA((PACK_PARTS, count)),
        ],
        compiler_params=pltpu.CompilerParams(vmem_limit_bytes=16 * 2**20),
        cost_estimate=pl.CostEstimate(flops=0, bytes_accessed=4 * size, transcendentals=0),
    )(index, x)


def routing(index, resident_count, block_count):
    owner = index // (resident_count * block_count)
    local = index % resident_count
    positions = jnp.arange(index.shape[-1], dtype=jnp.int32)
    same = owner[..., :, None] == owner[..., None, :]
    earlier = positions[None, :] < positions[:, None]
    rank = jnp.sum(jnp.where(same & earlier, 1, 0), axis=-1).astype(jnp.int32)
    return owner, local, rank


def padded_path(tokens, weight, down, up, index):
    wide_count = lax.axis_size("wide")
    req_count = index.shape[0]
    owner, local, rank = routing(index, down.shape[0], lax.axis_size("blk"))
    slot_count = wide_count * CAP
    base = jnp.dot(
        tokens,
        lax.all_gather(weight, "blk", axis=0, tiled=True),
        preferred_element_type=F32,
    )
    positions = jnp.arange(req_count, dtype=jnp.int32)
    slot_of_req = owner * CAP + rank
    member = slot_of_req[:, None] == jnp.arange(slot_count, dtype=jnp.int32)[None, :]
    source_req = jnp.sum(jnp.where(member, positions[:, None], 0), axis=0)
    slot_local = jnp.sum(jnp.where(member, local[:, None], 0), axis=0)[:, None]
    outgoing = take(tokens.reshape(req_count, SEQ, tokens.shape[1]), source_req)
    arrived = lax.all_to_all(outgoing, "wide", split_axis=0, concat_axis=0, tiled=True)
    ids = lax.all_to_all(slot_local, "wide", split_axis=0, concat_axis=0, tiled=True)[:, 0]
    shrink = jnp.einsum(
        "sqd,srd->sqr", arrived, take(down, ids), preferred_element_type=F32
    ).astype(BF16)
    expand = jnp.einsum(
        "sqr,srk->sqk", shrink, take(up, ids), preferred_element_type=F32
    ).astype(BF16)
    returned = lax.all_to_all(expand, "wide", split_axis=0, concat_axis=0, tiled=True)
    delta = take(returned, slot_of_req).reshape(tokens.shape[0], up.shape[2])
    return (base + delta.astype(F32)).astype(BF16)


def fused_kernel(
    n, m,
    ids_ref, slot_ref, tokens_hbm, pack_hbm, weight_hbm, down_hbm, up_hbm,
    out_ref,
    tokens, weight, down, up, arrived, total, delta, returned,
    local_sem, rx_send, rx_recv, fwd_send, ret_send, ret_recv,
    own_send, chain_send, chain_recv, mate_send, mate_recv, cross_send, cross_recv,
):
    w, p = lax.axis_index("wide"), lax.axis_index("blk")
    depth = weight_hbm.shape[0]
    half = depth // 2
    piece = half // PIECES
    width, columns = tokens.shape[1], out_ref.shape[1]
    reqs = slot_ref.shape[0]
    core = lax.rem(w, 2)

    def partner(j):
        bits = [lax.rem(w // (1 << i), 2) for i in range((n - 1).bit_length())]
        return sum(
            ((1 - bit) if (j >> i) & 1 else bit) * (1 << i) for i, bit in enumerate(bits)
        )

    mate = partner(1)

    locals_ = [
        pltpu.make_async_copy(
            weight_hbm,
            weight.at[pl.ds(pl.multiple_of(p * depth, depth), depth)],
            local_sem.at[0],
        ),
        pltpu.make_async_copy(tokens_hbm, tokens, local_sem.at[1]),
        pltpu.make_async_copy(down_hbm, down, local_sem.at[2]),
        pltpu.make_async_copy(up_hbm, up, local_sem.at[3]),
        pltpu.make_async_copy(pack_hbm.at[w], arrived.at[w], local_sem.at[4]),
        pltpu.make_async_copy(pack_hbm.at[n], arrived.at[n + w], local_sem.at[5]),
    ]

    barrier = pltpu.get_barrier_semaphore()
    for j in range(1, n):
        pl.semaphore_signal(barrier, inc=1, device_id=(partner(j), p), device_id_type=MESH)
    for q in (lax.rem(p + 1, m), lax.rem(p + m - 1, m)):
        pl.semaphore_signal(barrier, inc=1, device_id=(w, q), device_id_type=MESH)
    for copy in locals_:
        copy.start()
    pl.semaphore_wait(barrier, n + 1)

    def remote(src, dst, send, recv, device):
        return pltpu.make_async_remote_copy(
            src_ref=src, dst_ref=dst, send_sem=send, recv_sem=recv,
            device_id=device, device_id_type=MESH,
        )

    def rows(k, side, i):
        return pl.ds(pl.multiple_of(k * depth + side * half + i * piece, piece), piece)

    def own_copy(q, left, i):
        src = weight_hbm.at[pl.ds(pl.multiple_of(core * half + i * piece, piece), piece)]
        return remote(
            src, weight.at[rows(p, core, i)], own_send.at[left, i],
            chain_recv.at[p, i], (w, q),
        )

    def chain_copy(k, q, i):
        ref = weight.at[rows(k, core, i)]
        return remote(ref, ref, chain_send.at[k, i], chain_recv.at[k, i], (w, q))

    def mate_copy(k, side, i):
        ref = weight.at[rows(k, side, i)]
        return remote(ref, ref, mate_send.at[k, i], mate_recv.at[k, i], (mate, p))

    def slot_copy(j):
        q = partner(j)
        return remote(pack_hbm.at[q], arrived.at[w], rx_send.at[j], rx_recv.at[w], (q, p))

    def over_copy(j):
        return remote(
            pack_hbm.at[n], arrived.at[n + w], rx_send.at[n + j], rx_recv.at[n + w],
            (partner(j), p),
        )

    def cross_copy(i):
        near, far = (2, 4) if i == 0 else (4, 2)
        slot = n + partner(near)
        ref = arrived.at[slot, :, pl.ds(i * (width // 2), width // 2)]
        return remote(ref, ref, cross_send.at[i], cross_recv.at[i], (partner(far), p))

    def wait_cross(i):
        ref = arrived.at[n + partner(6), :, pl.ds(i * (width // 2), width // 2)]
        remote(ref, ref, cross_send.at[i], cross_recv.at[i], (mate, p)).wait_recv()

    def forward_copy(j):
        ref = arrived.at[n + partner(j)]
        return remote(ref, ref, fwd_send.at[j], rx_recv.at[n + partner(j)], (mate, p))

    def wait_rows(slot):
        remote(
            arrived.at[slot], arrived.at[slot], rx_send.at[0], rx_recv.at[slot], (mate, p)
        ).wait_recv()

    def return_copy(j, over):
        q = partner(j)
        return remote(
            delta.at[over * n + q], returned.at[over * n + w],
            ret_send.at[over * n + j], ret_recv.at[over * n + w], (q, p),
        )

    even = [j for j in range(2, n) if j % 2 == 0]
    odd = [j for j in range(2, n) if j % 2 == 1]

    @pl.when(p + 1 < m)
    def _():
        for i in range(PIECES):
            own_copy(p + 1, 0, i).start()

    @pl.when(p > 0)
    def _():
        for i in range(PIECES):
            own_copy(p - 1, 1, i).start()

    for j in (2, 4):
        over_copy(j).start()
    over_copy(1).start()
    slot_copy(1).start()
    for j in even:
        slot_copy(j).start()

    tile = 256

    def add_base(start, length):
        at = pl.ds(pl.multiple_of(start, 128), length)

        @pl.loop(0, columns // tile)
        def _(t):
            c = pl.ds(pl.multiple_of(t * tile, tile), tile)
            total[:, c] += jnp.dot(tokens[:, at], weight[at, c], preferred_element_type=F32)

    step = min(2048, width)

    def adapter(slot, out):
        a = ids_ref[slot]

        def body(c, acc):
            at = pl.ds(pl.multiple_of(c * step, step), step)
            return acc + lax.dot_general(
                arrived[slot, :, at], down[a, :, at], (((1,), (1,)), ((), ())),
                preferred_element_type=F32,
            )

        shrink = lax.fori_loop(
            0, width // step, body, jnp.zeros((SEQ, down.shape[1]), F32)
        ).astype(BF16)
        out[slot] = jnp.dot(shrink, up[a], preferred_element_type=F32).astype(BF16)

    def serve(j, over):
        adapter(over * n + partner(j), delta)
        return_copy(j, over).start()

    def ways(d):
        return (
            (p - d >= 0, p - d, p + 1 < m, p + 1),
            (p + d < m, p + d, p > 0, p - 1),
        )

    def chain(d):
        for i in range(PIECES):
            for exists, k, more, q in ways(d):

                @pl.when(exists)
                def _():
                    chain_copy(k, lax.rem(p + 1, m), i).wait_recv()

                    @pl.when(more)
                    def _():
                        chain_copy(k, q, i).start()

                    mate_copy(k, core, i).start()

    def chain_compute(d):
        for exists, k, _, _ in ways(d):

            @pl.when(exists)
            def _():
                add_base(k * depth + core * half, half)
                for i in range(PIECES):
                    mate_copy(k, 1 - core, i).wait_recv()
                add_base(k * depth + (1 - core) * half, half)

    total[...] = jnp.zeros_like(total)
    for i in (0, 1):
        locals_[i].wait()
    add_base(p * depth, half)
    add_base(p * depth + half, half)
    for i in (2, 3, 4, 5):
        locals_[i].wait()
    adapter(w, returned)
    adapter(n + w, returned)
    wait_rows(mate)
    serve(1, 0)
    wait_rows(n + mate)
    serve(1, 1)

    chain(1)
    for j in odd:
        slot_copy(j).start()
    chain_compute(1)
    for i, j in enumerate((2, 4)):
        wait_rows(n + partner(j))
        cross_copy(i).start()
        forward_copy(j).start()
    for j in (2, 4):
        serve(j, 1)
    if m > 2:
        chain(2)
        chain_compute(2)
    for i in (0, 1):
        wait_cross(i)
    forward_copy(6).start()
    serve(6, 1)
    for j in even:
        wait_rows(partner(j))
        serve(j, 0)
    for j in odd:
        wait_rows(n + partner(j))
        serve(j, 1)
    for j in odd:
        wait_rows(partner(j))
        serve(j, 0)

    @pl.loop(3, m)
    def _(d):
        chain(d)
        chain_compute(d)

    for over in (0, 1):
        for j in range(1, n):
            slot = over * n + partner(j)
            remote(
                delta.at[slot], returned.at[slot], ret_send.at[0], ret_recv.at[slot], (mate, p)
            ).wait_recv()

    @pl.loop(0, reqs)
    def _(r):
        at = pl.ds(pl.multiple_of(r * SEQ, SEQ), SEQ)
        out_ref[at] = (total[at] + returned[slot_ref[r]].astype(F32)).astype(out_ref.dtype)

    @pl.when(p + 1 < m)
    def _():
        for i in range(PIECES):
            own_copy(p + 1, 0, i).wait_send()

    @pl.when(p > 0)
    def _():
        for i in range(PIECES):
            own_copy(p - 1, 1, i).wait_send()

    @pl.loop(1, m)
    def _(d):
        for exists, k, more, q in ways(d):

            @pl.when(exists)
            def _():
                for i in range(PIECES):
                    mate_copy(k, core, i).wait_send()

                @pl.when(more)
                def _():
                    for i in range(PIECES):
                        chain_copy(k, q, i).wait_send()

    for j in range(1, n):
        slot_copy(j).wait_send()
        return_copy(j, 0).wait_send()
        return_copy(j, 1).wait_send()
    over_copy(1).wait_send()
    for i, j in enumerate((2, 4)):
        over_copy(j).wait_send()
        cross_copy(i).wait_send()
    for j in even:
        forward_copy(j).wait_send()


def fused_path(tokens, weight, down, up, pack, ids, slot_of_req):
    n, m = lax.axis_size("wide"), lax.axis_size("blk")
    rows, width = tokens.shape
    columns = weight.shape[1]
    any_spec = pl.BlockSpec(memory_space=pl.ANY)
    smem = pl.BlockSpec(memory_space=pltpu.SMEM)
    dma = pltpu.SemaphoreType.DMA
    return pl.pallas_call(
        functools.partial(fused_kernel, n, m),
        out_shape=jax.ShapeDtypeStruct((rows, columns), BF16),
        in_specs=[smem, smem] + [any_spec] * 5,
        out_specs=pl.BlockSpec(memory_space=pltpu.VMEM),
        scratch_shapes=[
            pltpu.VMEM((rows, width), BF16),
            pltpu.VMEM((width, columns), BF16),
            pltpu.VMEM(down.shape, BF16),
            pltpu.VMEM(up.shape, BF16),
            pltpu.VMEM((2 * n, SEQ, width), BF16),
            pltpu.VMEM((rows, columns), F32),
            pltpu.VMEM((2 * n, SEQ, columns), BF16),
            pltpu.VMEM((2 * n, SEQ, columns), BF16),
            dma((6,)), dma((2 * n,)), dma((2 * n,)), dma((n,)), dma((2 * n,)), dma((2 * n,)),
            dma((2, PIECES)), dma((m, PIECES)), dma((m, PIECES)), dma((m, PIECES)), dma((m, PIECES)),
            dma((2,)), dma((2,)),
        ],
        compiler_params=pltpu.CompilerParams(
            collective_id=0, has_side_effects=True, vmem_limit_bytes=60 * 2**20
        ),
    )(ids, slot_of_req, tokens, pack, weight, down, up)


def per_device(tokens, weight, down, up, index):
    n, m = lax.axis_size("wide"), lax.axis_size("blk")
    w, p = lax.axis_index("wide"), lax.axis_index("blk")
    req_count = index.shape[0]
    resident = down.shape[0]
    owner, local, rank = routing(index, resident, m)
    positions = jnp.arange(req_count, dtype=jnp.int32)
    first = (owner[:, None] == jnp.arange(n, dtype=jnp.int32)) & (rank == 0)[:, None]
    source = jnp.concatenate([
        jnp.sum(jnp.where(first, positions[:, None], 0), axis=0),
        jnp.max(jnp.where(rank == 1, positions, 0))[None],
    ]).astype(jnp.int32)
    pack = pack_rows(tokens.reshape(req_count, SEQ, tokens.shape[1]), source)

    everyone = lax.all_to_all(
        jnp.broadcast_to(index, (n * m, req_count)),
        ("wide", "blk"), split_axis=0, concat_axis=0, tiled=True,
    ).reshape(n, m, req_count)
    owners, locals_, ranks = routing(everyone, resident, m)
    fits = jnp.all(jnp.sum(ranks, axis=-1) <= 1)
    mine = (owners == w) & (jnp.arange(m, dtype=jnp.int32) == p)[None, :, None]
    ids = jnp.concatenate([
        jnp.sum(jnp.where(mine & (ranks == k), locals_, 0), axis=(1, 2)) for k in range(CAP)
    ]).astype(jnp.int32)
    return lax.cond(
        fits,
        lambda: fused_path(tokens, weight, down, up, pack, ids, owner + n * rank),
        lambda: padded_path(tokens, weight, down, up, index),
    )


def solution(mesh):
    return jax.shard_map(
        per_device,
        mesh=mesh,
        in_specs=(
            P(("wide", "blk"), None),
            P("blk", None),
            P(("wide", "blk"), None, None),
            P(("wide", "blk"), None, None),
            P(("wide", "blk")),
        ),
        out_specs=P(("wide", "blk"), None),
        check_vma=False,
    )
```
